128 devices in a mesh: ja: 8 (over x, core), ka: 16 (over z, y).
Axes of the slice: x: 4, y: 4, z: 4, core: 2. Of those that a mesh axis runs over, the one named last changes fastest.
Arguments:
- blocks: bfloat16 [512, 128, 128, 128], P(('ja', 'ka')), may hold values from -6 to 6
- coords: int32 [512, 3], P(('ja', 'ka')), may hold values from 0 to 127, as said below
- live_counts: int32 [128], P(('ja', 'ka')), may hold values from 1 to 4, as said below
- mode2_factor: bfloat16 [16384, 512], P(('ja', 'ka')), may hold values from -0.52734375 to 0.52734375
- mode3_factor: bfloat16 [16384, 512], P(('ka', 'ja')), may hold values from -0.52734375 to 0.52734375
Outputs:
- mttkrp: float32 [2048, 512], P(('ja', 'ka'))
The draws below stay inside these ranges and needn't reach their ends.
Inputs may be any that keep to these rules, and one draw needn't show every extreme that they name: `coords`: column 0 lies in 0 to 15 and favours some popular row blocks. The device at index j of ja and k of ka holds slots whose column 1 lies in j * 16 to (j + 1) * 16 - 1 and whose column 2 lies in k * 8 to (k + 1) * 8 - 1. `live_counts`: slots of a device beyond its count are dead; some device in every draw has all 4 slots live.
All inputs are finite; a program needn't handle non-finite values.
Results may differ from the reference program's by a relative error of at most 0.0003.
Values may be sent and summed in bfloat16 or wider, within the bound.
A program may use at most 64 MiB of HBM per device.

```python
import jax
import jax.numpy as jnp
from jax import lax

BS = 128
R = 512
BLK_DEV = 4
NI = 2048
NJ = 16384
NK = 16384
NBLK = 512
N_JA = 8
N_KA = 16
DEVICES = 128


def draw_coords(key, part):
    key_one, key_two, key_three, key_four, key_five = jax.random.split(jax.random.fold_in(key, 11), 5)
    row_blocks = NI // BS
    slot_index = jnp.arange(NBLK, dtype=jnp.int32)
    device = slot_index // BLK_DEV
    column = device // N_KA
    within = device % N_KA
    first = jax.random.randint(key_one, (NBLK,), 0, row_blocks, dtype=jnp.int32)
    second = jax.random.randint(key_two, (NBLK,), 0, row_blocks, dtype=jnp.int32)
    offset = jax.random.randint(key_three, (), 0, row_blocks, dtype=jnp.int32)
    mode1_block = (jnp.minimum(first, second) + offset) % row_blocks
    mode2_block = column * N_KA + jax.random.randint(key_four, (NBLK,), 0, N_KA, dtype=jnp.int32)
    mode3_block = within * N_JA + jax.random.randint(key_five, (NBLK,), 0, N_JA, dtype=jnp.int32)
    first_slot = slot_index == 0
    last_slot = slot_index == (DEVICES - 1) * BLK_DEV
    mode1_block = jnp.where(first_slot, 0, jnp.where(last_slot, row_blocks - 1, mode1_block))
    mode2_block = jnp.where(first_slot, 0, jnp.where(last_slot, DEVICES - 1, mode2_block))
    mode3_block = jnp.where(first_slot, 0, jnp.where(last_slot, DEVICES - 1, mode3_block))
    return jnp.stack([mode1_block, mode2_block, mode3_block], axis=1).astype(jnp.int32)


def draw_live_counts(key, part):
    key_one, key_two = jax.random.split(jax.random.fold_in(key, 23), 2)
    counts = jax.random.randint(key_one, (DEVICES,), 1, BLK_DEV + 1, dtype=jnp.int32)
    fullest = jax.random.randint(key_two, (), 0, DEVICES, dtype=jnp.int32)
    device = jnp.arange(DEVICES, dtype=jnp.int32)
    counts = jnp.where(device == (fullest + 1) % DEVICES, 1, counts)
    return jnp.where(device == fullest, BLK_DEV, counts).astype(jnp.int32)


def steps_of(own_key, extent, shards, smallest, high):
    def one(axis_at, shards_of):
        steps = jax.random.uniform(jax.random.fold_in(jax.random.fold_in(own_key, 6), axis_at), (shards_of,), jnp.float32, smallest / len(shards), high / len(shards))
        return jnp.repeat(jnp.exp(steps), extent[axis_at] // shards_of).reshape((-1,) + (1,) * (len(extent) - axis_at - 1))

    factor_of = one(*shards[0])
    for cut in shards[1:]:
        factor_of = factor_of * one(*cut)
    return factor_of


def centred(rng, dims, deviation, most, shards=(), kind=jnp.bfloat16):
    loudness = steps_of(rng, dims, shards, -0.22, 0.18) if shards else 1.0
    values = jax.random.normal(rng, dims, jnp.float32) * deviation * loudness
    return jnp.minimum(jnp.maximum(values, -most), most).astype(kind)


def setup_inputs(seed: int = 0) -> dict:
    key_list = jax.random.split(jax.random.key(seed), 6)
    blocks = centred(key_list[0], (NBLK, BS, BS, BS), 1.0, 6.0, ((0, 128),))
    coords = draw_coords(jax.random.fold_in(key_list[5], 71), 0)
    live_counts = draw_live_counts(jax.random.fold_in(key_list[5], 71), 0)
    mode2_factor = centred(key_list[3], (NJ, R), (BS ** -0.5), 0.52734375, ((0, 128),))
    mode3_factor = centred(key_list[4], (NK, R), (BS ** -0.5), 0.52734375, ((0, 128),))
    return {"blocks": blocks, "coords": coords, "live_counts": live_counts, "mode2_factor": mode2_factor, "mode3_factor": mode3_factor}


def accumulate(totals, block_cube, mode2_rows, mode3_rows, row_start):
    contracted = jnp.einsum("abc,cr->abr", block_cube, mode3_rows, preferred_element_type=jnp.float32)
    block_rows = jnp.einsum("abr,br->ar", contracted, mode2_rows.astype(jnp.float32))
    current = lax.dynamic_slice_in_dim(totals, row_start, block_rows.shape[0], 0)
    return lax.dynamic_update_slice_in_dim(totals, current + block_rows, row_start, 0)


def reference(blocks, coords, live_counts, mode2_factor, mode3_factor):
    block_edge = blocks.shape[1]
    totals = jnp.zeros((NI, R), jnp.float32)

    def add_block(running, slot_index):
        is_live = live_counts[slot_index // BLK_DEV] > slot_index % BLK_DEV

        def apply_block(current):
            position = coords[slot_index]
            block_cube = blocks[slot_index]
            mode2_rows = lax.dynamic_slice_in_dim(mode2_factor, (position[1] * block_edge).astype(jnp.int32), block_edge, 0)
            mode3_rows = lax.dynamic_slice_in_dim(mode3_factor, (position[2] * block_edge).astype(jnp.int32), block_edge, 0)
            return accumulate(current, block_cube, mode2_rows, mode3_rows, (position[0] * block_edge).astype(jnp.int32))

        return lax.cond(is_live, apply_block, lambda current: current, running), None

    totals, _ = lax.scan(add_block, totals, jnp.arange(NBLK, dtype=jnp.int32))
    return totals
```

```python
import functools

import jax
import jax.numpy as jnp
from jax import lax
from jax.experimental import pallas as pl
from jax.experimental.pallas import tpu as pltpu
from jax.sharding import PartitionSpec as P

MESH = pl.DeviceIdType.MESH

BS = 128
R = 512
SLOTS = 4
HALVES = 2
HC = R // HALVES
PHASES = 4
GROUPS = 2
TILES = 4
STEPS_PHASE = SLOTS * (8 // TILES)
SPACING = 3

GATHER2 = (("ya", "za", "yb", "zb"), ("za", "yb", "zb", "ya"), ("yb", "zb", "ya", "za"), ("zb", "ya", "za", "yb"))
GATHER3 = (("xa", "xb"), ("xb", "xa"))
SCATTER = (("xa", "ya", "za", "xb", "yb", "zb"), ("zb", "xb", "yb", "za", "xa", "ya"))
REDUCE_STEPS = 6
OFFSETS = (0, 32, 48, 56, 60, 62)


def flip_a(v, bit=1):
    return v + bit * (1 - 2 * (v % 2))


def flip_b(v, bit=1):
    return v + bit * (3 - 2 * v)


def place():
    ja = lax.axis_index("ja")
    ka = lax.axis_index("ka")
    return ja // 2, ja % 2, ka // 4, ka % 4


def partner(link):
    x, core, z, y = place()
    if link == "c":
        core = 1 - core
    elif link == "xa":
        x = flip_a(x)
    elif link == "xb":
        x = flip_b(x)
    elif link == "ya":
        y = flip_a(y)
    elif link == "yb":
        y = flip_b(y)
    elif link == "za":
        z = flip_a(z)
    else:
        z = flip_b(z)
    return (x * 2 + core, z * 4 + y)


def differing(v, w):
    low = (v + w) % 2
    high = (v // 2 + w // 2) % 2
    return (low + high) % 2, high


def kernel(
    blocks_ref, coords_ref, live_ref, mode2_ref, mode3_ref, out_ref,
    x_ref, p2a_ref, p2b_ref, p3a_ref, p3b_ref, w_ref, m_ref, rows_ref, meta_ref, sum_ref, got_ref,
    x_sem, send2, recv2, send3, recv3, send_meta, recv_meta, send_rows, recv_rows, send_sum, recv_sum,
):
    x, core, z, y = place()
    p2 = (p2a_ref, p2b_ref)
    p3 = (p3a_ref, p3b_ref)

    def block_copy(s):
        return pltpu.make_async_copy(blocks_ref.at[s], x_ref.at[s], x_sem.at[s])

    for s in range(SLOTS):
        block_copy(s).start()

    barrier = pltpu.get_barrier_semaphore()
    links = ("c", "xa", "xb", "ya", "yb", "za", "zb")
    for link in links:
        pl.semaphore_signal(barrier, inc=1, device_id=partner(link), device_id_type=MESH)

    for h in range(HALVES):
        for g in range(4):
            p2[h][g, 0] = mode2_ref[32 * g : 32 * (g + 1), HC * h : HC * (h + 1)]
        for g in range(2):
            p3[h][g, 0, 0] = mode3_ref[64 * g : 64 * (g + 1), HC * h : HC * (h + 1)]
    for s in range(SLOTS):
        mark = jnp.where(live_ref[0] > s, coords_ref[s, 0], -1).astype(jnp.float32)
        meta_ref[s] = jnp.full((8, 128), mark, jnp.float32)

    pl.semaphore_wait(barrier, len(links))

    def gather2(h, g, k):
        n = 1 << k
        return pltpu.make_async_remote_copy(
            src_ref=p2[h].at[g, pl.ds(0, n)], dst_ref=p2[h].at[g, pl.ds(n, n)],
            send_sem=send2.at[h, g, k], recv_sem=recv2.at[h, g, k],
            device_id=partner(GATHER2[g][k]), device_id_type=MESH,
        )

    def gather3(h, g, k):
        if k < 2:
            n = 1 << k
            src, dst = p3[h].at[g, 0, pl.ds(0, n)], p3[h].at[g, 0, pl.ds(n, n)]
            link = GATHER3[g][k]
        else:
            src, dst, link = p3[h].at[g, 0], p3[h].at[g, 1], "c"
        return pltpu.make_async_remote_copy(
            src_ref=src, dst_ref=dst, send_sem=send3.at[h, g, k], recv_sem=recv3.at[h, g, k],
            device_id=partner(link), device_id_type=MESH,
        )

    meta_copy = pltpu.make_async_remote_copy(
        src_ref=meta_ref.at[pl.ds(0, SLOTS)], dst_ref=meta_ref.at[pl.ds(SLOTS, SLOTS)],
        send_sem=send_meta, recv_sem=recv_meta, device_id=partner("c"), device_id_type=MESH,
    )

    for k in range(4):
        for h in range(HALVES):
            for g in range(4):
                if k > 0:
                    gather2(h, g, k - 1).wait_recv()
                gather2(h, g, k).start()
            if k < 3:
                for g in range(2):
                    if k > 0:
                        gather3(h, g, k - 1).wait_recv()
                    gather3(h, g, k).start()
    meta_copy.start()
    for s in range(SLOTS):
        block_copy(s).wait()

    def take_factors(h):
        for g in range(4):
            gather2(h, g, 3).wait_recv()
        for g in range(2):
            gather3(h, g, 2).wait_recv()
        for s in range(SLOTS):
            j = coords_ref[s, 1] % 16
            za, zb = differing(z, j // 4)
            ya, yb = differing(y, j % 4)
            bits = {"za": za, "zb": zb, "ya": ya, "yb": yb}
            for g in range(4):
                at = sum(bits[link] * (1 << k) for k, link in enumerate(GATHER2[g]))
                m_ref[s, 32 * g : 32 * (g + 1), :] = p2[h][g, at].astype(jnp.float32)
            i = coords_ref[s, 2] % 8
            xa, xb = differing(x, i // 2)
            other = (core + i % 2) % 2
            bits = {"xa": xa, "xb": xb}
            for g in range(2):
                at = sum(bits[link] * (1 << k) for k, link in enumerate(GATHER3[g]))
                w_ref[s, 64 * g : 64 * (g + 1), :] = p3[h][g, other, at]

    def rows_copy(phase, s):
        return pltpu.make_async_remote_copy(
            src_ref=rows_ref.at[phase, s], dst_ref=rows_ref.at[phase, SLOTS + s],
            send_sem=send_rows.at[phase, s], recv_sem=recv_rows.at[phase, s],
            device_id=partner("c"), device_id_type=MESH,
        )

    def compute(step):
        phase = step // STEPS_PHASE
        within = step % STEPS_PHASE
        s = within // (8 // TILES)
        first = (within % (8 // TILES)) * TILES
        for tile in range(TILES):
            u = first + tile
            lhs = x_ref[s, pl.ds(u * 16 + (phase % 2) * 8, 8)].reshape(8 * BS, BS)
            c = jnp.dot(lhs, w_ref[s], preferred_element_type=jnp.float32)
            c = (c.reshape(8, 16, 8, HC) * m_ref[s].reshape(1, 16, 8, HC)).sum(axis=1)
            rows_ref[phase, s, u] = c.sum(axis=1)

        @pl.when(within % (8 // TILES) == 8 // TILES - 1)
        def _():
            rows_copy(phase, s).start()

    def sum_copy(phase, g, k):
        n = 32 >> k
        return pltpu.make_async_remote_copy(
            src_ref=sum_ref.at[phase, g, pl.ds(n, n)], dst_ref=got_ref.at[phase, g, pl.ds(OFFSETS[k], n)],
            send_sem=send_sum.at[phase, g, k], recv_sem=recv_sum.at[phase, g, k],
            device_id=partner(SCATTER[g][k]), device_id_type=MESH,
        )

    def build(phase, g, upper):
        outer = [link for link in ("xa", "xb", "zb") if link != SCATTER[g][0]]
        weight = {link: 32 >> k for k, link in enumerate(SCATTER[g])}

        def one(m, _):
            bits = {SCATTER[g][0]: upper, outer[0]: m % 2, outer[1]: m // 2}
            x_to = flip_b(flip_a(x, bits["xa"]), bits["xb"])
            z_half = flip_b(z, bits["zb"])
            block = (x_to * 4 + core * 2 + z_half // 2).astype(jnp.float32)
            hits = [meta_ref[s] == block for s in range(2 * SLOTS)]
            base = sum(bits[link] * weight[link] for link in ("xa", "xb", "zb"))
            for za in range(2):
                z_to = flip_a(z_half, za)
                for yb in range(2):
                    for ya in range(2):
                        y_to = flip_b(flip_a(y, ya), yb)
                        u = (z_to % 2) * 4 + y_to
                        total = None
                        for s in range(2 * SLOTS):
                            term = jnp.where(hits[s], rows_ref[phase, s, u, :, 128 * g : 128 * (g + 1)], 0.0)
                            total = term if total is None else total + term
                        sum_ref[phase, g, base + za * weight["za"] + yb * weight["yb"] + ya * weight["ya"]] = total
            return 0

        lax.fori_loop(0, 4, one, 0)

    def event(e, phase):
        if e == 0:
            for s in range(SLOTS):
                rows_copy(phase, s).wait_recv()
            for g in range(GROUPS):
                build(phase, g, 1)
                sum_copy(phase, g, 0).start()
            for g in range(GROUPS):
                build(phase, g, 0)
            return
        n = 32 >> e
        for g in range(GROUPS):
            sum_copy(phase, g, e - 1).wait_recv()
            at = OFFSETS[e - 1]
            sum_ref[phase, g, n : 2 * n] = sum_ref[phase, g, n : 2 * n] + got_ref[phase, g, at + n : at + 2 * n]
            sum_copy(phase, g, e).start()
        for g in range(GROUPS):
            at = OFFSETS[e - 1]
            sum_ref[phase, g, 0:n] = sum_ref[phase, g, 0:n] + got_ref[phase, g, at : at + n]

    def one_step(step, _):
        for h in range(HALVES):
            @pl.when(step == h * 2 * STEPS_PHASE)
            def _():
                take_factors(h)
                if h == 0:
                    meta_copy.wait_recv()

        @pl.when(step < PHASES * STEPS_PHASE)
        def _():
            compute(step)

        for e in reversed(range(REDUCE_STEPS)):
            first = STEPS_PHASE + SPACING * e - 1
            after = step - first

            @pl.when((after >= 0) & (after < PHASES * STEPS_PHASE) & ((step + 8 * STEPS_PHASE - first) % STEPS_PHASE == 0))
            def _():
                event(e, (step + 8 * STEPS_PHASE - first) // STEPS_PHASE - 8)

        return 0

    total_steps = STEPS_PHASE * PHASES + SPACING * (REDUCE_STEPS - 1)
    lax.fori_loop(0, total_steps, one_step, 0)

    for phase in range(PHASES):
        for g in range(GROUPS):
            sum_copy(phase, g, REDUCE_STEPS - 1).wait_recv()
            h, t = phase // 2, phase % 2
            out_ref[8 * t : 8 * (t + 1), HC * h + 128 * g : HC * h + 128 * (g + 1)] = (
                sum_ref[phase, g, 0] + got_ref[phase, g, OFFSETS[-1]]
            )

    meta_copy.wait_send()
    for h in range(HALVES):
        for k in range(4):
            for g in range(4):
                gather2(h, g, k).wait_send()
        for k in range(3):
            for g in range(2):
                gather3(h, g, k).wait_send()

    def finish(phase, _):
        for s in range(SLOTS):
            rows_copy(phase, s).wait_send()
        for g in range(GROUPS):
            for k in range(REDUCE_STEPS):
                sum_copy(phase, g, k).wait_send()
        return 0

    lax.fori_loop(0, PHASES, finish, 0)


def on_device(blocks, coords, live_counts, mode2_factor, mode3_factor):
    dma = pltpu.SemaphoreType.DMA
    return pl.pallas_call(
        kernel,
        out_shape=jax.ShapeDtypeStruct((16, R), jnp.float32),
        in_specs=[
            pl.BlockSpec(memory_space=pl.ANY),
            pl.BlockSpec(memory_space=pltpu.SMEM),
            pl.BlockSpec(memory_space=pltpu.SMEM),
            pl.BlockSpec(memory_space=pltpu.VMEM),
            pl.BlockSpec(memory_space=pltpu.VMEM),
        ],
        out_specs=pl.BlockSpec(memory_space=pltpu.VMEM),
        scratch_shapes=[
            pltpu.VMEM((SLOTS, BS, BS, BS), jnp.bfloat16),
            pltpu.VMEM((4, 16, 32, HC), jnp.bfloat16),
            pltpu.VMEM((4, 16, 32, HC), jnp.bfloat16),
            pltpu.VMEM((2, 2, 4, 64, HC), jnp.bfloat16),
            pltpu.VMEM((2, 2, 4, 64, HC), jnp.bfloat16),
            pltpu.VMEM((SLOTS, BS, HC), jnp.bfloat16),
            pltpu.VMEM((SLOTS, BS, HC), jnp.float32),
            pltpu.VMEM((PHASES, 2 * SLOTS, 8, 8, HC), jnp.float32),
            pltpu.VMEM((2 * SLOTS, 8, 128), jnp.float32),
            pltpu.VMEM((PHASES, GROUPS, 64, 8, 128), jnp.float32),
            pltpu.VMEM((PHASES, GROUPS, 64, 8, 128), jnp.float32),
            dma((SLOTS,)),
            dma((HALVES, 4, 4)),
            dma((HALVES, 4, 4)),
            dma((HALVES, 2, 3)),
            dma((HALVES, 2, 3)),
            dma,
            dma,
            dma((PHASES, SLOTS)),
            dma((PHASES, SLOTS)),
            dma((PHASES, GROUPS, REDUCE_STEPS)),
            dma((PHASES, GROUPS, REDUCE_STEPS)),
        ],
        compiler_params=pltpu.CompilerParams(
            collective_id=0, has_side_effects=True, vmem_limit_bytes=48 * 2**20
        ),
        name="mttkrp",
    )(blocks, coords, live_counts, mode2_factor, mode3_factor)


def solution(mesh):
    placed = (
        P(("ja", "ka"), None, None, None),
        P(("ja", "ka"), None),
        P(("ja", "ka")),
        P(("ja", "ka"), None),
        P(("ka", "ja"), None),
    )
    return jax.shard_map(
        on_device, mesh=mesh, in_specs=placed, out_specs=P(("ja", "ka"), None), check_vma=False
    )
```

```python
import functools

import jax
import jax.numpy as jnp
from jax import lax
from jax.experimental import pallas as pl
from jax.experimental.pallas import tpu as pltpu
from jax.sharding import PartitionSpec as P

MESH = pl.DeviceIdType.MESH

BS = 128
R = 512
SLOTS = 4
HALVES = 2
HC = R // HALVES
PHASES = 4
GROUPS = 2
TILES = 4
EVENTS = ((2, 2, 2), (1, 2, 0), (0, 1, 1))
LEFT = ((1, 2), (0, 3), (2, 2), (1, 3), (2, 3))
GATHER_SLOTS = (0, 3)

GATHER2 = ("yz", "zy")
SCATTER = ("xyz", "zxy")
REDUCE_STEPS = 3
OFFSETS = (0, 48, 60)
RINGS = ("x1", "x2", "x3", "y1", "y2", "y3", "z1", "z2", "z3")


def place():
    ja = lax.axis_index("ja")
    ka = lax.axis_index("ka")
    return ja // 2, ja % 2, ka // 4, ka % 4


def partner_of(link, x, core, z, y):
    if link == "c":
        core = 1 - core
    else:
        up = int(link[1])
        if link[0] == "x":
            x = (x + up) % 4
        elif link[0] == "y":
            y = (y + up) % 4
        else:
            z = (z + up) % 4
    return (x * 2 + core, z * 4 + y)


def kernel(
    blocks_ref, coords_hbm, live_hbm, mode2_ref, mode3_ref, out_ref,
    coords_ref, live_ref, x_ref, p2a_ref, p2b_ref, p3a_ref, p3b_ref, w_ref, m_ref, rows_ref, meta_ref, sum_ref, got_ref,
    int_sem, own2_sem, own3_sem, x_sem, send2, recv2, send3, recv3, send_meta, recv_meta, send_rows, recv_rows, send_sum, recv_sum,
):
    x, core, z, y = place()
    links = ("c",) + RINGS
    partners = {link: partner_of(link, x, core, z, y) for link in links}
    partner = partners.get
    p2 = (p2a_ref, p2b_ref)
    p3 = (p3a_ref, p3b_ref)

    def block_copy(s):
        return pltpu.make_async_copy(blocks_ref.at[s], x_ref.at[s], x_sem.at[s])

    barrier = pltpu.get_barrier_semaphore()
    for link in links:
        pl.semaphore_signal(barrier, inc=1, device_id=partner(link), device_id_type=MESH)

    fetches = [
        pltpu.make_async_copy(coords_hbm, coords_ref, int_sem.at[0]),
        pltpu.make_async_copy(live_hbm, live_ref, int_sem.at[1]),
    ]

    def own2(h, g):
        return mode2_ref.at[pl.ds(64 * g, 64), pl.ds(HC * h, HC)]

    def own3(h):
        return mode3_ref.at[:, pl.ds(HC * h, HC)]

    own_copies = []
    for h in range(HALVES):
        for g in range(2):
            own_copies.append(pltpu.make_async_copy(own2(h, g), p2[h].at[g, 0, 0], own2_sem.at[h, g]))
        own_copies.append(pltpu.make_async_copy(own3(h), p3[h].at[0, 0], own3_sem.at[h]))
    for copy in fetches + own_copies:
        copy.start()

    def gather2(h, g, k, up):
        if k == 0:
            src, dst = own2(h, g), p2[h].at[g, 0, up]
        else:
            src, dst = p2[h].at[g, 0], p2[h].at[g, up]
        return pltpu.make_async_remote_copy(
            src_ref=src, dst_ref=dst, send_sem=send2.at[h, g, k, up - 1], recv_sem=recv2.at[h, g, k, up - 1],
            device_id=partner(GATHER2[g][k] + str(up)), device_id_type=MESH,
        )

    def gather3(h, up):
        if up > 0:
            src, dst, link = own3(h), p3[h].at[0, up], "x" + str(up)
        else:
            src, dst, link = p3[h].at[0], p3[h].at[1], "c"
        return pltpu.make_async_remote_copy(
            src_ref=src, dst_ref=dst, send_sem=send3.at[h, up], recv_sem=recv3.at[h, up],
            device_id=partner(link), device_id_type=MESH,
        )

    def gather_step(h, k):
        if k == 1:
            for g in range(2):
                for up in (1, 3, 2):
                    gather2(h, g, 0, up).wait_recv()
                for up in (2, 1, 3):
                    gather2(h, g, 1, up).start()
            for up in (1, 3, 2):
                gather3(h, up).wait_recv()
            gather3(h, 0).start()
            return
        for up in (2, 1, 3):
            for g in range(2):
                gather2(h, g, 0, up).start()
            gather3(h, up).start()

    pl.semaphore_wait(barrier, len(links))
    gather_step(0, 0)
    for s in range(SLOTS):
        block_copy(s).start()
    for copy in fetches + own_copies:
        copy.wait()
    for s in range(SLOTS):
        mark = jnp.where(live_ref[0] > s, coords_ref[s, 0], -1).astype(jnp.float32)
        meta_ref[s] = jnp.full((8, 128), mark, jnp.float32)

    meta_copy = pltpu.make_async_remote_copy(
        src_ref=meta_ref.at[pl.ds(0, SLOTS)], dst_ref=meta_ref.at[pl.ds(SLOTS, SLOTS)],
        send_sem=send_meta, recv_sem=recv_meta, device_id=partner("c"), device_id_type=MESH,
    )

    meta_copy.start()
    gather_step(0, 1)
    for s in range(SLOTS):
        block_copy(s).wait()

    def take_factors(h):
        for g in range(2):
            for up in (1, 3, 2):
                gather2(h, g, 1, up).wait_recv()
        gather3(h, 0).wait_recv()
        for s in range(SLOTS):
            j = coords_ref[s, 1] % 16
            back = {"z": (z - j // 4 + 4) % 4, "y": (y - j % 4 + 4) % 4}
            for g in range(2):
                first, second = GATHER2[g]
                m_ref[s, 64 * g : 64 * (g + 1), :] = p2[h][g, back[second], back[first]].astype(jnp.float32)
            i = coords_ref[s, 2] % 8
            w_ref[s] = p3[h][(core + i % 2) % 2, (x - i // 2 + 4) % 4]

    def rows_copy(phase, s):
        return pltpu.make_async_remote_copy(
            src_ref=rows_ref.at[phase, s], dst_ref=rows_ref.at[phase, SLOTS + s],
            send_sem=send_rows.at[phase, s], recv_sem=recv_rows.at[phase, s],
            device_id=partner("c"), device_id_type=MESH,
        )

    def compute(phase, s):
        def tiles(part, _):
            for tile in range(TILES):
                u = part * TILES + tile
                lhs = x_ref[s, pl.ds(u * 16 + (phase % 2) * 8, 8)].reshape(8 * BS, BS)
                c = jnp.dot(lhs, w_ref[s], preferred_element_type=jnp.float32)
                c = (c.reshape(8, 16, 8, HC) * m_ref[s].reshape(1, 16, 8, HC)).sum(axis=1)
                rows_ref[phase, s, u] = c.sum(axis=1)
            return 0

        lax.fori_loop(0, 8 // TILES, tiles, 0)
        rows_copy(phase, s).start()

    def sum_copy(phase, g, k, up):
        n = 16 >> (2 * k)
        return pltpu.make_async_remote_copy(
            src_ref=sum_ref.at[phase, g, pl.ds(n * up, n)],
            dst_ref=got_ref.at[phase, g, pl.ds(OFFSETS[k] + n * (up - 1), n)],
            send_sem=send_sum.at[phase, g, k, up - 1], recv_sem=recv_sum.at[phase, g, k, up - 1],
            device_id=partner(SCATTER[g][k] + str(up)), device_id_type=MESH,
        )

    def build(phase, g, up):
        first = SCATTER[g][0]
        weight = {axis: 16 >> (2 * k) for k, axis in enumerate(SCATTER[g])}

        def one(m, _):
            x_up, z_up = (up, m) if first == "x" else (m, up)
            z_to = (z + z_up) % 4
            block = (((x + x_up) % 4) * 4 + core * 2 + z_to // 2).astype(jnp.float32)
            hits = [meta_ref[s] == block for s in range(2 * SLOTS)]
            base = x_up * weight["x"] + z_up * weight["z"]
            for y_up in range(4):
                u = (z_to % 2) * 4 + (y + y_up) % 4
                total = None
                for s in range(2 * SLOTS):
                    term = jnp.where(hits[s], rows_ref[phase, s, u, :, 128 * g : 128 * (g + 1)], 0.0)
                    total = term if total is None else total + term
                sum_ref[phase, g, base + y_up * weight["y"]] = total
            return 0

        lax.fori_loop(0, 4, one, 0)

    def event(e, phase):
        if e == 0:
            for s in range(SLOTS):
                rows_copy(phase, s).wait_recv()
            for up in (2, 1, 3):
                for g in range(GROUPS):
                    build(phase, g, up)
                    sum_copy(phase, g, 0, up).start()
            for g in range(GROUPS):
                build(phase, g, 0)
            return
        n = 64 >> (2 * e)
        for g in range(GROUPS):
            for up in (1, 3, 2):
                sum_copy(phase, g, e - 1, up).wait_recv()
            at = OFFSETS[e - 1]

            def added(low, high):
                total = sum_ref[phase, g, low:high]
                for part in range(3):
                    total = total + got_ref[phase, g, at + part * n + low : at + part * n + high]
                sum_ref[phase, g, low:high] = total

            added(n // 4, n)
            for up in (2, 1, 3):
                sum_copy(phase, g, e, up).start()
            added(0, n // 4)

    def finish_sum(phase):
        h, t = phase // 2, phase % 2
        for g in range(GROUPS):
            for up in (1, 3, 2):
                sum_copy(phase, g, REDUCE_STEPS - 1, up).wait_recv()
            total = sum_ref[phase, g, 0]
            for part in range(3):
                total = total + got_ref[phase, g, OFFSETS[-1] + part]
            out_ref[8 * t : 8 * (t + 1), HC * h + 128 * g : HC * h + 128 * (g + 1)] = total

    def one_phase(phase, _):
        for h in range(HALVES):
            @pl.when(phase == 2 * h)
            def _():
                take_factors(h)
                if h == 0:
                    meta_copy.wait_recv()

        for s in range(SLOTS):
            for k, at in enumerate(GATHER_SLOTS):
                if at % SLOTS == s:
                    @pl.when(phase == at // SLOTS)
                    def _():
                        gather_step(1, k)

            for e, later, at in EVENTS:
                if at == s:
                    @pl.when(phase >= later)
                    def _():
                        event(e, phase - later)

            compute(phase, s)
        return 0

    lax.fori_loop(0, PHASES, one_phase, 0)
    for e, phase in LEFT:
        event(e, phase)
    for phase in range(PHASES):
        finish_sum(phase)

    meta_copy.wait_send()
    for h in range(HALVES):
        for up in range(1, 4):
            for k in range(2):
                for g in range(2):
                    gather2(h, g, k, up).wait_send()
        for up in range(4):
            gather3(h, up).wait_send()

    def finish(phase, _):
        for s in range(SLOTS):
            rows_copy(phase, s).wait_send()
        for g in range(GROUPS):
            for k in range(REDUCE_STEPS):
                for up in range(1, 4):
                    sum_copy(phase, g, k, up).wait_send()
        return 0

    lax.fori_loop(0, PHASES, finish, 0)


def on_device(blocks, coords, live_counts, mode2_factor, mode3_factor):
    dma = pltpu.SemaphoreType.DMA
    return pl.pallas_call(
        kernel,
        out_shape=jax.ShapeDtypeStruct((16, R), jnp.float32),
        in_specs=[
            pl.BlockSpec(memory_space=pltpu.HBM),
            pl.BlockSpec(memory_space=pltpu.HBM),
            pl.BlockSpec(memory_space=pltpu.HBM),
            pl.BlockSpec(memory_space=pltpu.HBM),
            pl.BlockSpec(memory_space=pltpu.HBM),
        ],
        out_specs=pl.BlockSpec(memory_space=pltpu.VMEM),
        scratch_shapes=[
            pltpu.SMEM((SLOTS, 3), jnp.int32),
            pltpu.SMEM((1,), jnp.int32),
            pltpu.VMEM((SLOTS, BS, BS, BS), jnp.bfloat16),
            pltpu.VMEM((2, 4, 4, 64, HC), jnp.bfloat16),
            pltpu.VMEM((2, 4, 4, 64, HC), jnp.bfloat16),
            pltpu.VMEM((2, 4, BS, HC), jnp.bfloat16),
            pltpu.VMEM((2, 4, BS, HC), jnp.bfloat16),
            pltpu.VMEM((SLOTS, BS, HC), jnp.bfloat16),
            pltpu.VMEM((SLOTS, BS, HC), jnp.float32),
            pltpu.VMEM((PHASES, 2 * SLOTS, 8, 8, HC), jnp.float32),
            pltpu.VMEM((2 * SLOTS, 8, 128), jnp.float32),
            pltpu.VMEM((PHASES, GROUPS, 64, 8, 128), jnp.float32),
            pltpu.VMEM((PHASES, GROUPS, 64, 8, 128), jnp.float32),
            dma((2,)),
            dma((HALVES, 2)),
            dma((HALVES,)),
            dma((SLOTS,)),
            dma((HALVES, 2, 2, 3)),
            dma((HALVES, 2, 2, 3)),
            dma((HALVES, 4)),
            dma((HALVES, 4)),
            dma,
            dma,
            dma((PHASES, SLOTS)),
            dma((PHASES, SLOTS)),
            dma((PHASES, GROUPS, REDUCE_STEPS, 3)),
            dma((PHASES, GROUPS, REDUCE_STEPS, 3)),
        ],
        compiler_params=pltpu.CompilerParams(
            collective_id=0, has_side_effects=True, vmem_limit_bytes=63 * 2**20
        ),
        name="mttkrp",
    )(blocks, coords, live_counts, mode2_factor, mode3_factor)


def solution(mesh):
    placed = (
        P(("ja", "ka"), None, None, None),
        P(("ja", "ka"), None),
        P(("ja", "ka")),
        P(("ja", "ka"), None),
        P(("ka", "ja"), None),
    )
    return jax.shard_map(
        on_device, mesh=mesh, in_specs=placed, out_specs=P(("ja", "ka"), None), check_vma=False
    )
```

```python
import functools

import jax
import jax.numpy as jnp
from jax import lax
from jax.experimental import pallas as pl
from jax.experimental.pallas import tpu as pltpu
from jax.sharding import PartitionSpec as P

MESH = pl.DeviceIdType.MESH

BS = 128
R = 512
SLOTS = 4
HALVES = 2
HC = R // HALVES
PHASES = 4
GROUPS = 2
TILES = 8
EVENTS = ((2, 2, 3), (1, 2, 1), (0, 1, 2))
LEFT = ((0, 3), (1, 2), (2, 2), (1, 3), (2, 3))
GATHER_SLOTS = (0, 3)

GATHER2 = ("yz", "zy")
SCATTER = ("xyz", "zxy")
REDUCE_STEPS = 3
OFFSETS = (0, 48, 60)
RINGS = ("x1", "x2", "x3", "y1", "y2", "y3", "z1", "z2", "z3")


def place():
    ja = lax.axis_index("ja")
    ka = lax.axis_index("ka")
    return ja // 2, ja % 2, ka // 4, ka % 4


def partner_of(link, x, core, z, y):
    if link == "c":
        core = 1 - core
    else:
        up = int(link[1])
        if link[0] == "x":
            x = (x + up) % 4
        elif link[0] == "y":
            y = (y + up) % 4
        else:
            z = (z + up) % 4
    return (x * 2 + core, z * 4 + y)


def kernel(
    blocks_ref, coords_hbm, live_hbm, mode2_ref, mode3_ref, out_ref,
    coords_ref, live_ref, x_ref, p2a_ref, p2b_ref, p3a_ref, p3b_ref, w_ref, m_ref, rows_ref, meta_ref, sum_ref, got_ref,
    int_sem, own2_sem, own3_sem, x_sem, send2, recv2, send3, recv3, send_meta, recv_meta, send_rows, recv_rows, send_sum, recv_sum,
):
    x, core, z, y = place()
    links = ("c",) + RINGS
    partners = {link: partner_of(link, x, core, z, y) for link in links}
    partner = partners.get
    p2 = (p2a_ref, p2b_ref)
    p3 = (p3a_ref, p3b_ref)

    def block_copy(s):
        return pltpu.make_async_copy(blocks_ref.at[s], x_ref.at[s], x_sem.at[s])

    barrier = pltpu.get_barrier_semaphore()
    for link in links:
        pl.semaphore_signal(barrier, inc=1, device_id=partner(link), device_id_type=MESH)

    fetches = [
        pltpu.make_async_copy(coords_hbm, coords_ref, int_sem.at[0]),
        pltpu.make_async_copy(live_hbm, live_ref, int_sem.at[1]),
    ]

    def own2(h, g):
        return mode2_ref.at[pl.ds(64 * g, 64), pl.ds(HC * h, HC)]

    def own3(h):
        return mode3_ref.at[:, pl.ds(HC * h, HC)]

    own_copies = []
    for h in range(HALVES):
        for g in range(2):
            own_copies.append(pltpu.make_async_copy(own2(h, g), p2[h].at[g, 0, 0], own2_sem.at[h, g]))
        own_copies.append(pltpu.make_async_copy(own3(h), p3[h].at[0, 0], own3_sem.at[h]))
    for copy in fetches + own_copies:
        copy.start()

    def gather2(h, g, k, up):
        if k == 0:
            src, dst = own2(h, g), p2[h].at[g, 0, up]
        else:
            src, dst = p2[h].at[g, 0], p2[h].at[g, up]
        return pltpu.make_async_remote_copy(
            src_ref=src, dst_ref=dst, send_sem=send2.at[h, g, k, up - 1], recv_sem=recv2.at[h, g, k, up - 1],
            device_id=partner(GATHER2[g][k] + str(up)), device_id_type=MESH,
        )

    def gather3(h, up):
        if up > 0:
            src, dst, link = own3(h), p3[h].at[0, up], "x" + str(up)
        else:
            src, dst, link = p3[h].at[0], p3[h].at[1], "c"
        return pltpu.make_async_remote_copy(
            src_ref=src, dst_ref=dst, send_sem=send3.at[h, up], recv_sem=recv3.at[h, up],
            device_id=partner(link), device_id_type=MESH,
        )

    def gather_step(h, k):
        if k == 1:
            for g in range(2):
                for up in (1, 3, 2):
                    gather2(h, g, 0, up).wait_recv()
                for up in (2, 1, 3):
                    gather2(h, g, 1, up).start()
            for up in (1, 3, 2):
                gather3(h, up).wait_recv()
            gather3(h, 0).start()
            return
        for up in (2, 1, 3):
            for g in range(2):
                gather2(h, g, 0, up).start()
            gather3(h, up).start()

    pl.semaphore_wait(barrier, len(links))
    gather_step(0, 0)
    for s in range(SLOTS):
        block_copy(s).start()
    for copy in fetches + own_copies:
        copy.wait()
    for s in range(SLOTS):
        mark = jnp.where(live_ref[0] > s, coords_ref[s, 0], -1).astype(jnp.float32)
        meta_ref[s] = jnp.full((8, 128), mark, jnp.float32)

    meta_copy = pltpu.make_async_remote_copy(
        src_ref=meta_ref.at[pl.ds(0, SLOTS)], dst_ref=meta_ref.at[pl.ds(SLOTS, SLOTS)],
        send_sem=send_meta, recv_sem=recv_meta, device_id=partner("c"), device_id_type=MESH,
    )

    meta_copy.start()
    gather_step(0, 1)
    for s in range(SLOTS):
        block_copy(s).wait()

    def take_factors(h):
        for g in range(2):
            for up in (1, 3, 2):
                gather2(h, g, 1, up).wait_recv()
        gather3(h, 0).wait_recv()
        for s in range(SLOTS):
            j = coords_ref[s, 1] % 16
            back = {"z": (z - j // 4 + 4) % 4, "y": (y - j % 4 + 4) % 4}
            for g in range(2):
                first, second = GATHER2[g]
                m_ref[s, 64 * g : 64 * (g + 1), :] = p2[h][g, back[second], back[first]].astype(jnp.float32)
            i = coords_ref[s, 2] % 8
            w_ref[s] = p3[h][(core + i % 2) % 2, (x - i // 2 + 4) % 4]

    def rows_copy(phase, s):
        return pltpu.make_async_remote_copy(
            src_ref=rows_ref.at[phase, s], dst_ref=rows_ref.at[phase, SLOTS + s],
            send_sem=send_rows.at[phase, s], recv_sem=recv_rows.at[phase, s],
            device_id=partner("c"), device_id_type=MESH,
        )

    def compute(phase, s):
        def tiles(part, _):
            for tile in range(TILES):
                u = part * TILES + tile
                lhs = x_ref[s, pl.ds(u * 16 + (phase % 2) * 8, 8)].reshape(8 * BS, BS)
                c = jnp.dot(lhs, w_ref[s], preferred_element_type=jnp.float32)
                c = (c.reshape(8, 16, 8, HC) * m_ref[s].reshape(1, 16, 8, HC)).sum(axis=1)
                rows_ref[phase, s, u] = c.sum(axis=1)
            return 0

        lax.fori_loop(0, 8 // TILES, tiles, 0)
        rows_copy(phase, s).start()

    def sum_copy(phase, g, k, up):
        n = 16 >> (2 * k)
        return pltpu.make_async_remote_copy(
            src_ref=sum_ref.at[phase, g, pl.ds(n * up, n)],
            dst_ref=got_ref.at[phase, g, pl.ds(OFFSETS[k] + n * (up - 1), n)],
            send_sem=send_sum.at[phase, g, k, up - 1], recv_sem=recv_sum.at[phase, g, k, up - 1],
            device_id=partner(SCATTER[g][k] + str(up)), device_id_type=MESH,
        )

    def build(phase, g, up):
        first = SCATTER[g][0]
        weight = {axis: 16 >> (2 * k) for k, axis in enumerate(SCATTER[g])}

        def one(m, _):
            x_up, z_up = (up, m) if first == "x" else (m, up)
            z_to = (z + z_up) % 4
            block = (((x + x_up) % 4) * 4 + core * 2 + z_to // 2).astype(jnp.float32)
            hits = [meta_ref[s] == block for s in range(2 * SLOTS)]
            base = x_up * weight["x"] + z_up * weight["z"]
            for y_up in range(4):
                u = (z_to % 2) * 4 + (y + y_up) % 4
                total = None
                for s in range(2 * SLOTS):
                    term = jnp.where(hits[s], rows_ref[phase, s, u, :, 128 * g : 128 * (g + 1)], 0.0)
                    total = term if total is None else total + term
                sum_ref[phase, g, base + y_up * weight["y"]] = total
            return 0

        lax.fori_loop(0, 4, one, 0)

    def event(e, phase):
        if e == 0:
            for s in range(SLOTS):
                rows_copy(phase, s).wait_recv()
            for up in (2, 1, 3):
                for g in range(GROUPS):
                    build(phase, g, up)
                    sum_copy(phase, g, 0, up).start()
            for g in range(GROUPS):
                build(phase, g, 0)
            return
        n = 64 >> (2 * e)
        for g in range(GROUPS):
            for up in (1, 3, 2):
                sum_copy(phase, g, e - 1, up).wait_recv()
            at = OFFSETS[e - 1]

            def added(low, high):
                total = sum_ref[phase, g, low:high]
                for part in range(3):
                    total = total + got_ref[phase, g, at + part * n + low : at + part * n + high]
                sum_ref[phase, g, low:high] = total

            added(n // 4, n)
            for up in (2, 1, 3):
                sum_copy(phase, g, e, up).start()
            added(0, n // 4)

    def finish_sum(phase):
        h, t = phase // 2, phase % 2
        for g in range(GROUPS):
            for up in (1, 3, 2):
                sum_copy(phase, g, REDUCE_STEPS - 1, up).wait_recv()
            total = sum_ref[phase, g, 0]
            for part in range(3):
                total = total + got_ref[phase, g, OFFSETS[-1] + part]
            out_ref[8 * t : 8 * (t + 1), HC * h + 128 * g : HC * h + 128 * (g + 1)] = total

    def one_phase(phase, _):
        for h in range(HALVES):
            @pl.when(phase == 2 * h)
            def _():
                take_factors(h)
                if h == 0:
                    meta_copy.wait_recv()

        for s in range(SLOTS):
            for k, at in enumerate(GATHER_SLOTS):
                if at % SLOTS == s:
                    @pl.when(phase == at // SLOTS)
                    def _():
                        gather_step(1, k)

            for e, later, at in EVENTS:
                if at == s:
                    @pl.when(phase >= later)
                    def _():
                        event(e, phase - later)

            compute(phase, s)
        return 0

    lax.fori_loop(0, PHASES, one_phase, 0)
    for e, phase in LEFT:
        event(e, phase)
    for phase in range(PHASES):
        finish_sum(phase)

    meta_copy.wait_send()
    for h in range(HALVES):
        for up in range(1, 4):
            for k in range(2):
                for g in range(2):
                    gather2(h, g, k, up).wait_send()
        for up in range(4):
            gather3(h, up).wait_send()

    def finish(phase, _):
        for s in range(SLOTS):
            rows_copy(phase, s).wait_send()
        for g in range(GROUPS):
            for k in range(REDUCE_STEPS):
                for up in range(1, 4):
                    sum_copy(phase, g, k, up).wait_send()
        return 0

    lax.fori_loop(0, PHASES, finish, 0)


def on_device(blocks, coords, live_counts, mode2_factor, mode3_factor):
    dma = pltpu.SemaphoreType.DMA
    return pl.pallas_call(
        kernel,
        out_shape=jax.ShapeDtypeStruct((16, R), jnp.float32),
        in_specs=[
            pl.BlockSpec(memory_space=pltpu.HBM),
            pl.BlockSpec(memory_space=pltpu.HBM),
            pl.BlockSpec(memory_space=pltpu.HBM),
            pl.BlockSpec(memory_space=pltpu.HBM),
            pl.BlockSpec(memory_space=pltpu.HBM),
        ],
        out_specs=pl.BlockSpec(memory_space=pltpu.VMEM),
        scratch_shapes=[
            pltpu.SMEM((SLOTS, 3), jnp.int32),
            pltpu.SMEM((1,), jnp.int32),
            pltpu.VMEM((SLOTS, BS, BS, BS), jnp.bfloat16),
            pltpu.VMEM((2, 4, 4, 64, HC), jnp.bfloat16),
            pltpu.VMEM((2, 4, 4, 64, HC), jnp.bfloat16),
            pltpu.VMEM((2, 4, BS, HC), jnp.bfloat16),
            pltpu.VMEM((2, 4, BS, HC), jnp.bfloat16),
            pltpu.VMEM((SLOTS, BS, HC), jnp.bfloat16),
            pltpu.VMEM((SLOTS, BS, HC), jnp.float32),
            pltpu.VMEM((PHASES, 2 * SLOTS, 8, 8, HC), jnp.float32),
            pltpu.VMEM((2 * SLOTS, 8, 128), jnp.float32),
            pltpu.VMEM((PHASES, GROUPS, 64, 8, 128), jnp.float32),
            pltpu.VMEM((PHASES, GROUPS, 64, 8, 128), jnp.float32),
            dma((2,)),
            dma((HALVES, 2)),
            dma((HALVES,)),
            dma((SLOTS,)),
            dma((HALVES, 2, 2, 3)),
            dma((HALVES, 2, 2, 3)),
            dma((HALVES, 4)),
            dma((HALVES, 4)),
            dma,
            dma,
            dma((PHASES, SLOTS)),
            dma((PHASES, SLOTS)),
            dma((PHASES, GROUPS, REDUCE_STEPS, 3)),
            dma((PHASES, GROUPS, REDUCE_STEPS, 3)),
        ],
        compiler_params=pltpu.CompilerParams(
            collective_id=0, has_side_effects=True, vmem_limit_bytes=63 * 2**20
        ),
        name="mttkrp",
    )(blocks, coords, live_counts, mode2_factor, mode3_factor)


def solution(mesh):
    placed = (
        P(("ja", "ka"), None, None, None),
        P(("ja", "ka"), None),
        P(("ja", "ka")),
        P(("ja", "ka"), None),
        P(("ka", "ja"), None),
    )
    return jax.shard_map(
        on_device, mesh=mesh, in_specs=placed, out_specs=P(("ja", "ka"), None), check_vma=False
    )
```
